256 devices in a mesh: wide: 128 (over y, z, x), narrow: 2 (over core).
Axes of the slice: x: 4, y: 4, z: 8, core: 2. Of those that a mesh axis runs over, the one named last changes fastest.
Arguments:
- genotypes: int32 [262144, 2048], P('wide', 'narrow'), may hold values from 0 to 2
- allele_means: float32 [2048], P('narrow'), may hold values from 0.6 to 1.4
- allele_scales: float32 [2048], P('narrow'), may hold values from 0.4 to 4
- test_matrix: bfloat16 [2048, 128], P('narrow'), may hold values from -0.125 to 0.125
Outputs:
- scaled_basis: float32 [262144, 128], P('wide')
- projection: float32 [2048, 128], P('narrow')
The draws below stay inside these ranges and needn't reach their ends.
All inputs are finite; a program needn't handle non-finite values.
Results may differ from the reference program's by a relative error of at most 0.0003.
The reference program's roundings to bfloat16 on the way (of `standard` and `basis_low`) count: a program that leaves them out, or rounds other values in their place, can miss the bound.
Values sent between devices are 32-bit elements; how exact they have to be, the bound alone decides.
A program may use at most 64 MiB of HBM per device.

```python
import math
import jax
import jax.numpy as jnp
from jax import lax

RANK = 128
SAMPLES = 262144
VARIANTS = 2048


def touch_ends(array, key, smallest, top_value):
    longest = array.shape.index(max(array.shape))
    spots = []
    for shift in (0, 1):
        where = [jax.random.randint(jax.random.fold_in(key, axis), (), 0, length) for axis, length in enumerate(array.shape)]
        where[longest] = (where[longest] + shift) % array.shape[longest]
        spots.append(tuple(where))
    return array.at[spots[0]].set(smallest).at[spots[1]].set(top_value)


def levels(key, dims, shards, low, top_value):
    def one(position, parts):
        draws = jax.random.uniform(jax.random.fold_in(jax.random.fold_in(key, 6), position), (parts,), jnp.float32, low / len(shards), top_value / len(shards))
        return jnp.repeat(jnp.exp(draws), dims[position] // parts).reshape((-1,) + (1,) * (len(dims) - position - 1))

    gain = one(*shards[0])
    for cut in shards[1:]:
        gain = gain * one(*cut)
    return gain


def gaussian(rng, dims, scale, limit, pieces=(), held_as=jnp.bfloat16):
    entries = jax.random.normal(rng, dims, jnp.float32) * scale
    if len(pieces) > 0:
        entries = levels(rng, dims, pieces, -0.22, 0.18) * entries
    return jnp.clip(entries, min=-limit, max=limit).astype(held_as)


def setup_inputs(seed: int = 0) -> dict:
    keys = jax.random.split(jax.random.key(seed), 5)
    genotypes = touch_ends(jax.random.randint(keys[0], (SAMPLES, VARIANTS), 0, 3), jax.random.fold_in(keys[0], 1), 0, 2).astype(jnp.int32)
    allele_means = jnp.clip(0.6 + 0.79999995 * jax.random.uniform(keys[1], (VARIANTS,), jnp.float32) ** levels(keys[1], (VARIANTS,), ((0, 2),), -0.2, 0.2), 0.6, 1.4)
    allele_scales = jnp.clip(jnp.exp(math.log(4.0) - 2.3025851 * jax.random.uniform(keys[2], (VARIANTS,), jnp.float32) ** levels(keys[2], (VARIANTS,), ((0, 2),), -0.2, 0.2)), 0.4, 4.0)
    test_matrix = gaussian(keys[3], (VARIANTS, RANK), VARIANTS ** -0.5, 0.125, ((0, 2),))
    return dict(genotypes=genotypes, allele_means=allele_means, allele_scales=allele_scales, test_matrix=test_matrix)


def reference(genotypes, allele_means, allele_scales, test_matrix):
    standard = ((genotypes.astype(jnp.float32) - allele_means[None, :]) * allele_scales[None, :]).astype(jnp.bfloat16)
    sketch = jnp.dot(standard.astype(jnp.float32), test_matrix.astype(jnp.float32), preferred_element_type=jnp.float32)
    gram = lax.dot_general(sketch, sketch, (((0,), (0,)), ((), ())), precision=lax.Precision.HIGHEST)
    lower = jnp.linalg.cholesky(gram)
    basis = jax.scipy.linalg.solve_triangular(lower, sketch.T, lower=True).T
    scaled_basis = basis * jnp.sqrt(jnp.float32(SAMPLES))
    basis_low = basis.astype(jnp.bfloat16)
    projection = lax.dot_general(standard.astype(jnp.float32), basis_low.astype(jnp.float32), (((0,), (0,)), ((), ())), preferred_element_type=jnp.float32)
    return (scaled_basis, projection)
```

```python
import functools

import jax
import jax.numpy as jnp
from jax import lax
from jax.experimental import pallas as pl
from jax.experimental.pallas import tpu as pltpu
from jax.sharding import PartitionSpec as P

NX, NY, NZ = 4, 4, 8
RANK = 128
LAG = 2
F32, BF16 = jnp.float32, jnp.bfloat16
MESH = pl.DeviceIdType.MESH
HIGHEST = lax.Precision.HIGHEST


class Place:
    def __init__(self):
        w = lax.axis_index("wide")
        self.w = w
        self.c = lax.axis_index("narrow")
        self.x = lax.rem(w, NX)
        self.z = lax.rem(lax.div(w, NX), NZ)
        self.y = lax.div(w, NX * NZ)
        self.p = self.y * NX + self.x

    def plane(self, dy, dx):
        yy, xx = lax.rem(self.y + dy, NY), lax.rem(self.x + dx, NX)
        return yy, xx, (yy * NZ + self.z) * NX + xx

    def column(self, dz):
        zz = lax.rem(self.z + dz, NZ)
        return zz, (self.y * NZ + zz) * NX + self.x


def plane_steps():
    return [(dy, dx) for dy in range(NY) for dx in range(NX)]


def far_first(n):
    return sorted(range(n), key=lambda d: -min(d, n - d))


def id_of(wide, narrow):
    return {"wide": wide, "narrow": narrow}


def remote(src, dst, send, recv, device):
    copy = pltpu.make_async_remote_copy(
        src_ref=src, dst_ref=dst, send_sem=send, recv_sem=recv, device_id=device, device_id_type=MESH
    )
    copy.start()
    return copy


def sketch_kernel(
    gen, mean, scale, test, std, sketch, gram,
    gbuf, part, other, mine, r1, r2, total,
    gsem, ps, pr, s1, v1, s2, v2, s3, v3,
):
    me = Place()
    n_chunks = gsem.shape[0]
    rows = gbuf.shape[0] // n_chunks
    plane = NX * NY
    piece = mine.shape[1]

    loads = []
    for k in range(n_chunks):
        at = pl.ds(k * rows, rows)
        copy = pltpu.make_async_copy(gen.at[at], gbuf.at[at], gsem.at[k])
        copy.start()
        loads.append(copy)

    barrier = pltpu.get_barrier_semaphore()
    pl.semaphore_signal(barrier, inc=1, device_id=id_of(me.w, 1 - me.c), device_id_type=MESH)
    for dy, dx in plane_steps()[1:]:
        _, _, w = me.plane(dy, dx)
        for core in range(2):
            pl.semaphore_signal(barrier, inc=1, device_id=id_of(w, core), device_id_type=MESH)
    for dz in range(1, NZ):
        _, w = me.column(dz)
        pl.semaphore_signal(barrier, inc=1, device_id=id_of(w, me.c), device_id_type=MESH)

    pairs = []
    acc = jnp.zeros((RANK, RANK), F32)
    for k in range(n_chunks + LAG):
        if k < n_chunks:
            at = pl.ds(k * rows, rows)
            loads[k].wait()
            std[at, :] = ((gbuf[at, :].astype(F32) - mean[...]) * scale[...]).astype(BF16)
            part[at, :] = jnp.dot(std[at, :], test[...], preferred_element_type=F32)
            if k == 0:
                pl.semaphore_wait(barrier, 1 + 2 * (plane - 1) + NZ - 1)
            pairs.append(remote(part.at[at], other.at[at], ps.at[k], pr.at[k], id_of(me.w, 1 - me.c)))
        if k >= LAG:
            at = pl.ds((k - LAG) * rows, rows)
            pairs[k - LAG].wait_recv()
            s = part[at, :] + other[at, :]
            sketch[at, :] = s
            acc += lax.dot_general(s, s, (((0,), (0,)), ((), ())), precision=HIGHEST, preferred_element_type=F32)

    for i in range(RANK // piece):
        mine[i] = acc[i * piece : (i + 1) * piece, :]
    sends = list(pairs)

    recvs = []
    for dy, dx in [(dy, dx) for dy in far_first(NY) for dx in far_first(NX)][:-1]:
        yy, xx, w = me.plane(dy, dx)
        s = dy * NX + dx
        recvs.append(remote(mine.at[plane * me.c + yy * NX + xx], r1.at[s], s1.at[s], v1.at[s], id_of(w, me.c)))
    t = mine[plane * me.c + me.p]
    for copy in recvs:
        copy.wait_recv()
    sends += recvs
    for s in range(1, plane):
        t += r1[s]
    r2[me.z] = t
    recvs = []
    for dz in far_first(NZ)[:-1]:
        _, w = me.column(dz)
        recvs.append(remote(r2.at[me.z], r2.at[me.z], s2.at[dz], v2.at[dz], id_of(w, me.c)))
    for copy in recvs:
        copy.wait_recv()
    sends += recvs
    t = r2[0]
    for i in range(1, NZ):
        t += r2[i]
    slot = plane * me.c + me.p
    total[slot] = t
    recvs = []
    for dy, dx in [(dy, dx) for dy in far_first(NY) for dx in far_first(NX)]:
        _, _, w = me.plane(dy, dx)
        for dc in range(2):
            s = (dy * NX + dx) * 2 + dc
            if s:
                core = me.c if dc == 0 else 1 - me.c
                recvs.append(remote(total.at[slot], total.at[slot], s3.at[s], v3.at[s], id_of(w, core)))
    for copy in recvs:
        copy.wait_recv()
    sends += recvs
    for i in range(RANK // piece):
        gram[i * piece : (i + 1) * piece, :] = total[i]
    for copy in sends:
        copy.wait_send()


def split3(v):
    hi = v.astype(BF16)
    rest = v - hi.astype(F32)
    mid = rest.astype(BF16)
    low = (rest - mid.astype(F32)).astype(BF16)
    return hi, mid, low


PANEL = 16


def inverse_factor(gram_ref, aug):
    n = RANK
    row = lax.broadcasted_iota(jnp.int32, (n, n), 0)
    col = lax.broadcasted_iota(jnp.int32, (n, n), 1)
    aug[:, :n] = gram_ref[...]
    aug[:, n:] = jnp.where(row == col, 1.0, 0.0).astype(F32)
    prow = lax.broadcasted_iota(jnp.int32, (PANEL, n), 0)
    prow2 = lax.broadcasted_iota(jnp.int32, (PANEL, 2 * n), 0)
    for k in range(n // PANEL):
        base = k * PANEL
        p = aug[base : base + PANEL, :]
        cols = [jnp.broadcast_to(p[:, base + j : base + j + 1], (PANEL, n)) for j in range(PANEL)]
        diag = jnp.zeros((PANEL, n), F32)
        for i in range(PANEL):
            pivot = cols[i][i : i + 1, :]
            diag = jnp.where(prow == i, pivot, diag)
            if i == PANEL - 1:
                break
            m = jnp.where(prow > i, cols[i] * (1.0 / pivot), 0.0)
            for j in range(i + 1, PANEL):
                cols[j] = cols[j] - m * cols[j][i : i + 1, :]
            m2 = jnp.concatenate([m, m], axis=1)
            p = p - m2 * p[i : i + 1, :]
        r = 1.0 / jnp.sqrt(diag)
        u = p * jnp.concatenate([r, r], axis=1)
        aug[base : base + PANEL, :] = u
        if base + PANEL < n:
            h, m, l = split3(u)
            left = jnp.concatenate([h, h, m, h, l, m], axis=0)[:, :n]
            right = jnp.concatenate([h, m, h, l, h, m], axis=0)
            upd = lax.dot_general(left, right, (((0,), (0,)), ((), ())), preferred_element_type=F32)
            aug[base + PANEL :, :] = aug[base + PANEL :, :] - upd[base + PANEL :, :]


def basis_kernel(factor, gram, sketch, scaled, low, aug):
    inverse_factor(gram, aug)
    w = aug[:, RANK:]
    basis = lax.dot_general(
        sketch[...], w, (((1,), (1,)), ((), ())), precision=HIGHEST, preferred_element_type=F32
    )
    scaled[...] = basis * factor
    low[...] = basis.astype(BF16)


def projection_kernel(std, low, out, mine, ra, sb, rb, sa, va, s2, v2, s3, v3, s4, v4):
    me = Place()
    plane = NX * NY
    piece = mine.shape[2]
    block = NX * piece
    barrier = pltpu.get_barrier_semaphore()
    for dy, dx in plane_steps()[1:]:
        _, _, w = me.plane(dy, dx)
        pl.semaphore_signal(barrier, inc=1, device_id=id_of(w, me.c), device_id_type=MESH)
    for dz in range(1, NZ):
        _, w = me.column(dz)
        pl.semaphore_signal(barrier, inc=1, device_id=id_of(w, me.c), device_id_type=MESH)

    sends, recvs = [], []
    lowt = low[...].T
    for i, dy in enumerate(far_first(NY)):
        yy = lax.rem(me.y + dy, NY)
        at = pl.ds(pl.multiple_of(yy * block, block), block)
        res = jnp.dot(lowt, std[:, at], preferred_element_type=F32)
        mine[dy] = res.T.reshape(NX, piece, RANK)
        if i == 0:
            pl.semaphore_wait(barrier, plane - 1 + NZ - 1)
        for dx in far_first(NX):
            s = dy * NX + dx
            if s:
                _, xx, w = me.plane(dy, dx)
                recvs.append(remote(mine.at[dy, xx], ra.at[s], sa.at[s], va.at[s], id_of(w, me.c)))
    t = mine[0, me.x]
    for copy in recvs:
        copy.wait_recv()
    sends += recvs
    for s in range(1, plane):
        t += ra[s]
    zp = piece // NZ
    sb[...] = t.reshape(NZ, zp, RANK)
    recvs = []
    for dz in far_first(NZ)[:-1]:
        zz, w = me.column(dz)
        recvs.append(remote(sb.at[zz], rb.at[dz], s2.at[dz], v2.at[dz], id_of(w, me.c)))
    t = sb[me.z]
    for copy in recvs:
        copy.wait_recv()
    sends += recvs
    for s in range(1, NZ):
        t += rb[s]
    first = me.p * piece
    own = pl.ds(pl.multiple_of(first + me.z * zp, zp), zp)
    out[own, :] = t
    recvs = []
    for dz in far_first(NZ)[:-1]:
        _, w = me.column(dz)
        recvs.append(remote(out.at[own], out.at[own], s3.at[dz], v3.at[dz], id_of(w, me.c)))
    for copy in recvs:
        copy.wait_recv()
    sends += recvs
    whole = pl.ds(pl.multiple_of(first, piece), piece)
    recvs = []
    for dy, dx in [(dy, dx) for dy in far_first(NY) for dx in far_first(NX)][:-1]:
        _, _, w = me.plane(dy, dx)
        s = dy * NX + dx
        recvs.append(remote(out.at[whole], out.at[whole], s4.at[s], v4.at[s], id_of(w, me.c)))
    for copy in recvs:
        copy.wait_recv()
    sends += recvs
    for copy in sends:
        copy.wait_send()


CHUNKS = 8


def body(genotypes, allele_means, allele_scales, test_matrix):
    samples, variants = genotypes.shape
    plane = NX * NY
    dma = pltpu.SemaphoreType.DMA
    vmem = pl.BlockSpec(memory_space=pltpu.VMEM)
    piece = RANK // 2 // plane
    std, sketch, gram = pl.pallas_call(
        sketch_kernel,
        out_shape=(
            jax.ShapeDtypeStruct((samples, variants), BF16),
            jax.ShapeDtypeStruct((samples, RANK), F32),
            jax.ShapeDtypeStruct((RANK, RANK), F32),
        ),
        in_specs=[pl.BlockSpec(memory_space=pltpu.HBM), vmem, vmem, vmem],
        out_specs=(vmem, vmem, vmem),
        scratch_shapes=[
            pltpu.VMEM((samples, variants), jnp.int32),
            pltpu.VMEM((samples, RANK), F32),
            pltpu.VMEM((samples, RANK), F32),
            pltpu.VMEM((RANK // piece, piece, RANK), F32),
            pltpu.VMEM((plane, piece, RANK), F32),
            pltpu.VMEM((NZ, piece, RANK), F32),
            pltpu.VMEM((RANK // piece, piece, RANK), F32),
            dma((CHUNKS,)), dma((CHUNKS,)), dma((CHUNKS,)),
            dma((plane,)), dma((plane,)), dma((NZ,)), dma((NZ,)),
            dma((2 * plane,)), dma((2 * plane,)),
        ],
        compiler_params=pltpu.CompilerParams(
            collective_id=0, has_side_effects=True, vmem_limit_bytes=40 << 20
        ),
        name="sketch_gram",
    )(genotypes, allele_means[None, :], allele_scales[None, :], test_matrix)

    factor = float(samples * lax.axis_size("wide")) ** 0.5
    scaled, low = pl.pallas_call(
        functools.partial(basis_kernel, factor),
        out_shape=(
            jax.ShapeDtypeStruct((samples, RANK), F32),
            jax.ShapeDtypeStruct((samples, RANK), BF16),
        ),
        in_specs=[vmem, vmem],
        out_specs=(vmem, vmem),
        scratch_shapes=[pltpu.VMEM((RANK, 2 * RANK), F32)],
        compiler_params=pltpu.CompilerParams(vmem_limit_bytes=40 << 20),
        name="factor_basis",
    )(gram, sketch)

    piece = variants // plane
    projection = pl.pallas_call(
        projection_kernel,
        out_shape=jax.ShapeDtypeStruct((variants, RANK), F32),
        in_specs=[vmem, vmem],
        out_specs=vmem,
        scratch_shapes=[
            pltpu.VMEM((NY, NX, piece, RANK), F32),
            pltpu.VMEM((plane, piece, RANK), F32),
            pltpu.VMEM((NZ, piece // NZ, RANK), F32),
            pltpu.VMEM((NZ, piece // NZ, RANK), F32),
            dma((plane,)), dma((plane,)), dma((NZ,)), dma((NZ,)),
            dma((NZ,)), dma((NZ,)), dma((plane,)), dma((plane,)),
        ],
        compiler_params=pltpu.CompilerParams(
            collective_id=1, has_side_effects=True, vmem_limit_bytes=40 << 20
        ),
        name="projection",
    )(std, low)
    return scaled, projection


def solution(mesh):
    in_specs = (P("wide", "narrow"), P("narrow"), P("narrow"), P("narrow", None))
    out_specs = (P("wide", None), P("narrow", None))
    return jax.shard_map(body, mesh=mesh, in_specs=in_specs, out_specs=out_specs, check_vma=False)
```

```python
import functools

import jax
import jax.numpy as jnp
from jax import lax
from jax.experimental import pallas as pl
from jax.experimental.pallas import tpu as pltpu
from jax.sharding import PartitionSpec as P

NX, NY, NZ = 4, 4, 8
RANK = 128
CHUNKS = 8
EARLY = 5
LAG = 2
PANEL = 16
F32, BF16 = jnp.float32, jnp.bfloat16
MESH = pl.DeviceIdType.MESH
HIGHEST = lax.Precision.HIGHEST


class Place:
    def __init__(self):
        w = lax.axis_index("wide")
        self.w = w
        self.c = lax.axis_index("narrow")
        self.x = lax.rem(w, NX)
        self.z = lax.rem(lax.div(w, NX), NZ)
        self.y = lax.div(w, NX * NZ)
        self.p = self.y * NX + self.x

    def plane(self, dy, dx):
        yy, xx = lax.rem(self.y + dy, NY), lax.rem(self.x + dx, NX)
        return yy * NX + xx, {"wide": (yy * NZ + self.z) * NX + xx, "narrow": self.c}

    def column(self, dz):
        zz = lax.rem(self.z + dz, NZ)
        return zz, {"wide": (self.y * NZ + zz) * NX + self.x, "narrow": self.c}


def far_first(n):
    return sorted(range(n), key=lambda d: -min(d, n - d))


def plane_steps():
    steps = [(dy * NX + dx, dy, dx) for dy in range(NY) for dx in range(NX)]
    return sorted(steps, key=lambda s: -min(s[1], NY - s[1]) - min(s[2], NX - s[2]))[:-1]


def near_first(n):
    return far_first(n)[::-1]


def remote(src, dst, send, recv, device):
    copy = pltpu.make_async_remote_copy(
        src_ref=src, dst_ref=dst, send_sem=send, recv_sem=recv, device_id=device, device_id_type=MESH
    )
    copy.start()
    return copy


def split3(v):
    hi = v.astype(BF16)
    rest = v - hi.astype(F32)
    mid = rest.astype(BF16)
    low = (rest - mid.astype(F32)).astype(BF16)
    return hi, mid, low


def inverse_factor(aug):
    n = RANK
    prow = lax.broadcasted_iota(jnp.int32, (PANEL, n), 0)
    for k in range(n // PANEL):
        base = k * PANEL
        p = aug[base : base + PANEL, :]
        cols = [jnp.broadcast_to(p[:, base + j : base + j + 1], (PANEL, n)) for j in range(PANEL)]
        diag = jnp.zeros((PANEL, n), F32)
        for i in range(PANEL):
            pivot = cols[i][i : i + 1, :]
            diag = jnp.where(prow == i, pivot, diag)
            if i == PANEL - 1:
                break
            m = jnp.where(prow > i, cols[i] * (1.0 / pivot), 0.0)
            for j in range(i + 1, PANEL):
                cols[j] = cols[j] - m * cols[j][i : i + 1, :]
            p = p - jnp.concatenate([m, m], axis=1) * p[i : i + 1, :]
        r = 1.0 / jnp.sqrt(diag)
        u = p * jnp.concatenate([r, r], axis=1)
        aug[base : base + PANEL, :] = u
        if base + PANEL < n:
            h, m, l = split3(u)
            left = jnp.concatenate([h, h, m, h, l, m], axis=0)[:, :n]
            right = jnp.concatenate([h, m, h, l, h, m], axis=0)
            upd = lax.dot_general(left, right, (((0,), (0,)), ((), ())), preferred_element_type=F32)
            aug[base + PANEL :, :] = aug[base + PANEL :, :] - upd[base + PANEL :, :]


def main_kernel(
    factor,
    gen, mean_hbm, scale_hbm, test_hbm, scaled, out,
    gbuf, mean, scale, test, std, part, other, sketch,
    gm, r1, r2, total, aug, pm, pa, sb, rb,
    gsem, osem, ps, pr, s1, v1, s2, v2, s3, v3, s4, v4, s5, v5, s6, v6, s7, v7,
):
    me = Place()
    rows = gbuf.shape[0] // CHUNKS
    plane = NX * NY
    steps = plane_steps()
    partner = {"wide": me.w, "narrow": 1 - me.c}

    loads, operands, sends = [], [], []
    for i, (src, dst) in enumerate(((mean_hbm, mean), (scale_hbm, scale), (test_hbm, test))):
        copy = pltpu.make_async_copy(src, dst, osem.at[i])
        copy.start()
        operands.append(copy)
    for k in range(CHUNKS):
        at = pl.ds(k * rows, rows)
        copy = pltpu.make_async_copy(gen.at[at], gbuf.at[at], gsem.at[k])
        copy.start()
        loads.append(copy)

    barrier = pltpu.get_barrier_semaphore()
    for device in [me.plane(dy, dx)[1] for _, dy, dx in steps] + [
        me.column(dz)[1] for dz in far_first(NZ)[:-1]
    ] + [partner]:
        pl.semaphore_signal(barrier, inc=1, device_id=device, device_id_type=MESH)

    for copy in operands:
        copy.wait()
    pairs = []
    acc = jnp.zeros((RANK, RANK), F32)

    def exchange(k):
        at = pl.ds(k * rows, rows)
        pairs.append(remote(part.at[at], other.at[at], ps.at[k], pr.at[k], partner))

    def combine(k):
        at = pl.ds(k * rows, rows)
        pairs[k].wait_recv()
        s = part[at, :] + other[at, :]
        sketch[at, :] = s
        return lax.dot_general(s, s, (((0,), (0,)), ((), ())), precision=HIGHEST, preferred_element_type=F32)

    done = 0
    for k in range(CHUNKS):
        at = pl.ds(k * rows, rows)
        loads[k].wait()
        x = ((gbuf[at, :].astype(F32) - mean[...]) * scale[...]).astype(BF16)
        std[at, :] = x
        part[at, :] = jnp.dot(x, test[...], preferred_element_type=F32)
        if k == EARLY - 1:
            pl.semaphore_wait(barrier, plane - 1 + NZ - 1 + 1)
            for i in range(EARLY):
                exchange(i)
        elif k >= EARLY:
            exchange(k)
            if k - done >= LAG:
                acc += combine(done)
                done += 1
    while done < CHUNKS:
        acc += combine(done)
        done += 1
    sends += pairs

    gm[...] = acc.reshape(gm.shape)
    recvs = []
    for s, dy, dx in steps:
        q, device = me.plane(dy, dx)
        recvs.append(remote(gm.at[q], r1.at[s], s1.at[s], v1.at[s], device))
    t = gm[me.p]
    for copy in recvs:
        copy.wait_recv()
    sends += recvs
    for s in range(1, plane):
        t += r1[s]
    r2[me.z] = t
    recvs = []
    for dz in far_first(NZ)[:-1]:
        _, device = me.column(dz)
        recvs.append(remote(r2.at[me.z], r2.at[me.z], s2.at[dz], v2.at[dz], device))
    for copy in recvs:
        copy.wait_recv()
    sends += recvs
    t = r2[0]
    for i in range(1, NZ):
        t += r2[i]
    total[me.p] = t
    recvs = []
    for s, dy, dx in steps:
        _, device = me.plane(dy, dx)
        recvs.append(remote(total.at[me.p], total.at[me.p], s3.at[s], v3.at[s], device))
    row = lax.broadcasted_iota(jnp.int32, (RANK, RANK), 0)
    col = lax.broadcasted_iota(jnp.int32, (RANK, RANK), 1)
    aug[:, RANK:] = jnp.where(row == col, 1.0, 0.0).astype(F32)
    for copy in recvs:
        copy.wait_recv()
    sends += recvs
    aug[:, :RANK] = total[...].reshape(RANK, RANK)

    inverse_factor(aug)
    basis = lax.dot_general(
        sketch[...], aug[:, RANK:], (((1,), (1,)), ((), ())), precision=HIGHEST, preferred_element_type=F32
    )
    scaled[...] = basis * factor
    lowt = basis.astype(BF16).T

    order = near_first(NZ)
    half = NZ // 2
    stage = {}
    for g in (1, 0):
        for j in range(g * half, g * half + half, 2):
            blocks = []
            for jj in (j, j + 1):
                zz, _ = me.column(order[jj])
                blocks.append(std[:, pl.ds(pl.multiple_of(zz * RANK, RANK), RANK)])
            res = jnp.dot(lowt, jnp.concatenate(blocks, axis=1), preferred_element_type=F32).T
            pm[:, j] = res[:RANK].reshape(plane, -1, RANK)
            pm[:, j + 1] = res[RANK:].reshape(plane, -1, RANK)
        at = pl.ds(g * half, half)
        stage[g] = []
        for s, dy, dx in steps:
            q, device = me.plane(dy, dx)
            stage[g].append(remote(pm.at[q, at], pa.at[s, at], s4.at[g, s], v4.at[g, s], device))
        sends += stage[g]
    recvs = []
    for g in (1, 0):
        at = pl.ds(g * half, half)
        t = pm[me.p, at]
        for copy in stage[g]:
            copy.wait_recv()
        for s in range(1, plane):
            t += pa[s, at]
        sb[at] = t
        for j in reversed(range(max(1, g * half), g * half + half)):
            _, device = me.column(order[j])
            recvs.append(remote(sb.at[j], rb.at[j], s5.at[j], v5.at[j], device))
    for copy in recvs:
        copy.wait_recv()
    sends += recvs
    t = sb[0]
    for j in range(1, NZ):
        t += rb[j]
    out[me.p, 0] = t
    recvs = [None] * NZ
    for dz in far_first(NZ)[:-1]:
        j = order.index((NZ - dz) % NZ)
        _, device = me.column(dz)
        recvs[j] = remote(out.at[me.p, 0], out.at[me.p, j], s6.at[j], v6.at[j], device)
    sends += recvs[1:]
    last = []
    for g in (0, 1):
        at = pl.ds(g * half, half)
        for copy in recvs[max(1, g * half) : g * half + half]:
            copy.wait_recv()
        for s, dy, dx in steps:
            _, device = me.plane(dy, dx)
            last.append(remote(out.at[me.p, at], out.at[me.p, at], s7.at[g, s], v7.at[g, s], device))
    for copy in last:
        copy.wait_recv()
    sends += last
    for copy in sends:
        copy.wait_send()


def place_kernel(scaled_in, slots, scaled, projection):
    scaled[...] = scaled_in[...]
    me = Place()
    n = slots.shape[0] * slots.shape[2]
    for j, dz in enumerate(near_first(NZ)):
        zz, _ = me.column(dz)
        projection[pl.ds(pl.multiple_of(zz * n, n), n), :] = slots[:, j].reshape(n, RANK)


def body(genotypes, allele_means, allele_scales, test_matrix):
    samples, variants = genotypes.shape
    plane = NX * NY
    dma = pltpu.SemaphoreType.DMA
    vmem = pl.BlockSpec(memory_space=pltpu.VMEM)
    piece = variants // (plane * NZ)
    factor = float(samples * lax.axis_size("wide")) ** 0.5
    grow = RANK // plane
    operands = (genotypes, allele_means[None, :], allele_scales[None, :], test_matrix)
    operands = [pltpu.with_memory_space_constraint(v, pltpu.HBM) for v in operands]
    scaled, slots = pl.pallas_call(
        functools.partial(main_kernel, factor),
        out_shape=(
            jax.ShapeDtypeStruct((samples, RANK), F32),
            jax.ShapeDtypeStruct((plane, NZ, piece, RANK), F32),
        ),
        in_specs=[pl.BlockSpec(memory_space=pltpu.HBM)] * 4,
        out_specs=(vmem, vmem),
        scratch_shapes=[
            pltpu.VMEM((samples, variants), jnp.int32),
            pltpu.VMEM((1, variants), F32),
            pltpu.VMEM((1, variants), F32),
            pltpu.VMEM((variants, RANK), BF16),
            pltpu.VMEM((samples, variants), BF16),
            pltpu.VMEM((samples, RANK), F32),
            pltpu.VMEM((samples, RANK), F32),
            pltpu.VMEM((samples, RANK), F32),
            pltpu.VMEM((plane, grow, RANK), F32),
            pltpu.VMEM((plane, grow, RANK), F32),
            pltpu.VMEM((NZ, grow, RANK), F32),
            pltpu.VMEM((plane, grow, RANK), F32),
            pltpu.VMEM((RANK, 2 * RANK), F32),
            pltpu.VMEM((plane, NZ, piece, RANK), F32),
            pltpu.VMEM((plane, NZ, piece, RANK), F32),
            pltpu.VMEM((NZ, piece, RANK), F32),
            pltpu.VMEM((NZ, piece, RANK), F32),
            dma((CHUNKS,)), dma((3,)), dma((CHUNKS,)), dma((CHUNKS,)),
            dma((plane,)), dma((plane,)), dma((NZ,)), dma((NZ,)), dma((plane,)), dma((plane,)),
            dma((2, plane)), dma((2, plane)), dma((NZ,)), dma((NZ,)),
            dma((NZ,)), dma((NZ,)), dma((2, plane)), dma((2, plane)),
        ],
        compiler_params=pltpu.CompilerParams(
            collective_id=0, has_side_effects=True, vmem_limit_bytes=40 << 20
        ),
        name="sketch_factor_project",
    )(*operands)
    return pl.pallas_call(
        place_kernel,
        out_shape=(
            jax.ShapeDtypeStruct((samples, RANK), F32),
            jax.ShapeDtypeStruct((variants, RANK), F32),
        ),
        in_specs=[vmem, vmem],
        out_specs=(vmem, vmem),
        compiler_params=pltpu.CompilerParams(vmem_limit_bytes=40 << 20),
        name="place",
    )(scaled, slots)


def solution(mesh):
    in_specs = (P("wide", "narrow"), P("narrow"), P("narrow"), P("narrow", None))
    out_specs = (P("wide", None), P("narrow", None))
    return jax.shard_map(body, mesh=mesh, in_specs=in_specs, out_specs=out_specs, check_vma=False)
```

```python
import functools

import jax
import jax.numpy as jnp
from jax import lax
from jax.experimental import pallas as pl
from jax.experimental.pallas import tpu as pltpu
from jax.sharding import PartitionSpec as P

NX, NY, NZ = 4, 4, 8
RANK = 128
CHUNKS = 4
EARLY = 3
LAG = 2
BLOCKS = 4
AHEAD = 4
PANEL = 16
F32, BF16 = jnp.float32, jnp.bfloat16
MESH = pl.DeviceIdType.MESH
HIGHEST = lax.Precision.HIGHEST


class Place:
    def __init__(self):
        w = lax.axis_index("wide")
        self.w = w
        self.c = lax.axis_index("narrow")
        self.x = lax.rem(w, NX)
        self.z = lax.rem(lax.div(w, NX), NZ)
        self.y = lax.div(w, NX * NZ)
        self.p = self.y * NX + self.x

    def plane(self, dy, dx):
        yy, xx = lax.rem(self.y + dy, NY), lax.rem(self.x + dx, NX)
        return yy * NX + xx, {"wide": (yy * NZ + self.z) * NX + xx, "narrow": self.c}

    def column(self, dz):
        zz = lax.rem(self.z + dz, NZ)
        return zz, {"wide": (self.y * NZ + zz) * NX + self.x, "narrow": self.c}


def hops(d, n):
    return min(d, n - d)


def far_first(n):
    return sorted(range(n), key=lambda d: -hops(d, n))


def plane_steps():
    steps = [(dy * NX + dx, dy, dx) for dy in range(NY) for dx in range(NX)]
    return sorted(steps, key=lambda s: -hops(s[1], NY) - hops(s[2], NX))[:-1]


def remote(src, dst, send, recv, device):
    copy = pltpu.make_async_remote_copy(
        src_ref=src, dst_ref=dst, send_sem=send, recv_sem=recv, device_id=device, device_id_type=MESH
    )
    copy.start()
    return copy


def wait_bytes(ref, sem):
    pltpu.make_async_copy(ref, ref, sem).wait()


def split3(v):
    hi = v.astype(BF16)
    rest = v - hi.astype(F32)
    mid = rest.astype(BF16)
    low = (rest - mid.astype(F32)).astype(BF16)
    return hi, mid, low


def inverse_factor(aug):
    n = RANK
    prow = lax.broadcasted_iota(jnp.int32, (PANEL, n), 0)
    for k in range(n // PANEL):
        base = k * PANEL
        p = aug[base : base + PANEL, :]
        cols = [jnp.broadcast_to(p[:, base + j : base + j + 1], (PANEL, n)) for j in range(PANEL)]
        diag = jnp.zeros((PANEL, n), F32)
        for i in range(PANEL):
            pivot = cols[i][i : i + 1, :]
            diag = jnp.where(prow == i, pivot, diag)
            if i == PANEL - 1:
                break
            m = jnp.where(prow > i, cols[i] * (1.0 / pivot), 0.0)
            for j in range(i + 1, PANEL):
                cols[j] = cols[j] - m * cols[j][i : i + 1, :]
            p = p - jnp.concatenate([m, m], axis=1) * p[i : i + 1, :]
        r = 1.0 / jnp.sqrt(diag)
        u = p * jnp.concatenate([r, r], axis=1)
        aug[base : base + PANEL, :] = u
        if base + PANEL < n:
            h, m, l = split3(u)
            left = jnp.concatenate([h, h, m, h, l, m], axis=0)[:, :n]
            right = jnp.concatenate([h, m, h, l, h, m], axis=0)
            upd = lax.dot_general(left, right, (((0,), (0,)), ((), ())), preferred_element_type=F32)
            aug[base + PANEL :, :] = aug[base + PANEL :, :] - upd[base + PANEL :, :]


def main_kernel(
    factor,
    gen, mean_hbm, scale_hbm, test_hbm, scaled, out,
    gbuf, mean, scale, test, std, part, other, sketch,
    gm, r1, r2, total, aug, pm, pa, zb,
    gsem, osem, ps, pr, ss, rs, sa, va, sb, vb, sc, vc,
):
    me = Place()
    rows = gbuf.shape[0] // CHUNKS
    plane = NX * NY
    steps = plane_steps()
    partner = {"wide": me.w, "narrow": 1 - me.c}

    loads = []

    def load(first, last):
        for i in range(first, last):
            if i < 3:
                src, dst = ((mean_hbm, mean), (scale_hbm, scale), (test_hbm, test))[i]
                copy = pltpu.make_async_copy(src, dst, osem.at[i])
            else:
                at = pl.ds((i - 3) * rows, rows)
                copy = pltpu.make_async_copy(gen.at[at], gbuf.at[at], gsem.at[i - 3])
            copy.start()
            loads.append(copy)

    load(0, AHEAD)
    barrier = pltpu.get_barrier_semaphore()
    peers = [(hops(dy, NY) + hops(dx, NX), me.plane(dy, dx)[1]) for _, dy, dx in steps]
    peers += [(hops(dz, NZ), me.column(dz)[1]) for dz in range(1, NZ)] + [(0, partner)]
    for _, device in sorted(peers, key=lambda p: -p[0]):
        pl.semaphore_signal(barrier, inc=1, device_id=device, device_id_type=MESH)
    load(AHEAD, 3 + CHUNKS)

    for copy in loads[:3]:
        copy.wait()
    pairs = []
    acc = [jnp.zeros((2 * RANK, 2 * RANK), F32), jnp.zeros((RANK, RANK), F32)]

    def exchange(k):
        at = pl.ds(k * rows, rows)
        pairs.append(remote(part.at[at], other.at[at], ps.at[k], pr.at[k], partner))

    def combine(k):
        at = pl.ds(k * rows, rows)
        pairs[k].wait_recv()
        s = part[at, :] + other[at, :]
        sketch[at, :] = s
        h, m, l = split3(s)
        hm = jnp.concatenate([h, m], axis=1)
        acc[0] += lax.dot_general(hm, hm, (((0,), (0,)), ((), ())), preferred_element_type=F32)
        acc[1] += lax.dot_general(l, h, (((0,), (0,)), ((), ())), preferred_element_type=F32)

    done = 0
    for k in range(CHUNKS):
        at = pl.ds(k * rows, rows)
        loads[3 + k].wait()
        x = ((gbuf[at, :].astype(F32) - mean[...]) * scale[...]).astype(BF16)
        std[at, :] = x
        part[at, :] = jnp.dot(x, test[...], preferred_element_type=F32)
        if k == EARLY - 1:
            pl.semaphore_wait(barrier, plane - 1 + NZ - 1 + 1)
            for i in range(EARLY):
                exchange(i)
        elif k >= EARLY:
            exchange(k)
            if k - done >= LAG:
                combine(done)
                done += 1
    while done < CHUNKS:
        combine(done)
        done += 1

    a, b = acc
    a = a[:RANK, :RANK] + ((a[:RANK, RANK:] + a[RANK:, :RANK]) + (a[RANK:, RANK:] + (b + b.T)))
    gm[...] = a.reshape(gm.shape)
    for s, dy, dx in steps:
        q, device = me.plane(dy, dx)
        remote(gm.at[q], r1.at[s], ss.at[0], rs.at[0], device)
    t = gm[me.p]
    for copy in pairs:
        copy.wait_send()
    wait_bytes(r1.at[pl.ds(1, plane - 1)], rs.at[0])
    for s in range(1, plane):
        t += r1[s]
    r2[me.z] = t
    for dz in far_first(NZ)[:-1]:
        _, device = me.column(dz)
        remote(r2.at[me.z], r2.at[me.z], ss.at[1], rs.at[1], device)
    wait_bytes(gm.at[pl.ds(0, plane - 1)], ss.at[0])
    wait_bytes(r2.at[pl.ds(0, NZ - 1)], rs.at[1])
    t = r2[0]
    for i in range(1, NZ):
        t += r2[i]
    total[me.p] = t
    for s, dy, dx in steps:
        _, device = me.plane(dy, dx)
        remote(total.at[me.p], total.at[me.p], ss.at[2], rs.at[2], device)
    wait_bytes(r2.at[pl.ds(0, NZ - 1)], ss.at[1])
    row = lax.broadcasted_iota(jnp.int32, (RANK, RANK), 0)
    col = lax.broadcasted_iota(jnp.int32, (RANK, RANK), 1)
    aug[:, RANK:] = jnp.where(row == col, 1.0, 0.0).astype(F32)
    wait_bytes(total.at[pl.ds(0, plane - 1)], rs.at[2])
    aug[:, :RANK] = total[...].reshape(RANK, RANK)

    wait_bytes(total.at[pl.ds(0, plane - 1)], ss.at[2])

    inverse_factor(aug)
    basis = lax.dot_general(
        sketch[...], aug[:, RANK:], (((1,), (1,)), ((), ())), precision=HIGHEST, preferred_element_type=F32
    )
    scaled[...] = basis * factor
    lowt = basis.astype(BF16).T

    width = std.shape[1] // BLOCKS
    grow = width // plane
    for i in range(BLOCKS):
        res = jnp.dot(lowt, std[:, i * width : (i + 1) * width], preferred_element_type=F32)
        pm[i] = res.T.reshape(plane, grow, RANK)
        for s, dy, dx in steps:
            q, device = me.plane(dy, dx)
            remote(pm.at[i, q], pa.at[i, s], sa.at[i], va.at[i], device)
    for i in range(BLOCKS):
        t = pm[i, me.p]
        wait_bytes(pa.at[i, pl.ds(1, plane - 1)], va.at[i])
        for s in range(1, plane):
            t += pa[i, s]
        zb[i, me.z] = t
        for dz in far_first(NZ)[:-1]:
            _, device = me.column(dz)
            remote(zb.at[i, me.z], zb.at[i, me.z], sb.at[i], vb.at[i], device)
    for i in range(BLOCKS):
        wait_bytes(pm.at[i, pl.ds(0, plane - 1)], sa.at[i])
    for i in range(BLOCKS):
        wait_bytes(zb.at[i, pl.ds(0, NZ - 1)], vb.at[i])
        t = zb[i, 0]
        for z in range(1, NZ):
            t += zb[i, z]
        out[i, me.p] = t
        for s, dy, dx in steps:
            _, device = me.plane(dy, dx)
            remote(out.at[i, me.p], out.at[i, me.p], sc.at[i], vc.at[i], device)
    for i in range(BLOCKS):
        wait_bytes(zb.at[i, pl.ds(0, NZ - 1)], sb.at[i])
    for i in range(BLOCKS):
        wait_bytes(out.at[i, pl.ds(0, plane - 1)], sc.at[i])
        wait_bytes(out.at[i, pl.ds(0, plane - 1)], vc.at[i])


def place_kernel(scaled_in, projection_in, scaled, projection, sems):
    copies = [
        pltpu.make_async_copy(scaled_in, scaled, sems.at[0]),
        pltpu.make_async_copy(projection_in, projection, sems.at[1]),
    ]
    for copy in copies:
        copy.start()
    for copy in copies:
        copy.wait()


def body(genotypes, allele_means, allele_scales, test_matrix):
    samples, variants = genotypes.shape
    plane = NX * NY
    dma = pltpu.SemaphoreType.DMA
    vmem = pl.BlockSpec(memory_space=pltpu.VMEM)
    piece = variants // (plane * BLOCKS)
    factor = float(samples * lax.axis_size("wide")) ** 0.5
    grow = RANK // plane
    operands = (genotypes, allele_means[None, :], allele_scales[None, :], test_matrix)
    operands = [pltpu.with_memory_space_constraint(v, pltpu.HBM) for v in operands]
    scaled, projection = pl.pallas_call(
        functools.partial(main_kernel, factor),
        out_shape=(
            jax.ShapeDtypeStruct((samples, RANK), F32),
            jax.ShapeDtypeStruct((BLOCKS, plane, piece, RANK), F32),
        ),
        in_specs=[pl.BlockSpec(memory_space=pltpu.HBM)] * 4,
        out_specs=(vmem, vmem),
        scratch_shapes=[
            pltpu.VMEM((samples, variants), jnp.int32),
            pltpu.VMEM((1, variants), F32),
            pltpu.VMEM((1, variants), F32),
            pltpu.VMEM((variants, RANK), BF16),
            pltpu.VMEM((samples, variants), BF16),
            pltpu.VMEM((samples, RANK), F32),
            pltpu.VMEM((samples, RANK), F32),
            pltpu.VMEM((samples, RANK), F32),
            pltpu.VMEM((plane, grow, RANK), F32),
            pltpu.VMEM((plane, grow, RANK), F32),
            pltpu.VMEM((NZ, grow, RANK), F32),
            pltpu.VMEM((plane, grow, RANK), F32),
            pltpu.VMEM((RANK, 2 * RANK), F32),
            pltpu.VMEM((BLOCKS, plane, piece, RANK), F32),
            pltpu.VMEM((BLOCKS, plane, piece, RANK), F32),
            pltpu.VMEM((BLOCKS, NZ, piece, RANK), F32),
            dma((CHUNKS,)), dma((3,)), dma((CHUNKS,)), dma((CHUNKS,)),
            dma((3,)), dma((3,)), dma((BLOCKS,)), dma((BLOCKS,)),
            dma((BLOCKS,)), dma((BLOCKS,)), dma((BLOCKS,)), dma((BLOCKS,)),
        ],
        compiler_params=pltpu.CompilerParams(
            collective_id=0, has_side_effects=True, vmem_limit_bytes=40 << 20
        ),
        name="sketch_factor_project",
    )(*operands)
    return pl.pallas_call(
        place_kernel,
        out_shape=(
            jax.ShapeDtypeStruct((samples, RANK), F32),
            jax.ShapeDtypeStruct((variants, RANK), F32),
        ),
        in_specs=[vmem, vmem],
        out_specs=(pl.BlockSpec(memory_space=pltpu.HBM), pl.BlockSpec(memory_space=pltpu.HBM)),
        scratch_shapes=[dma((2,))],
        compiler_params=pltpu.CompilerParams(vmem_limit_bytes=4 << 20),
        name="place",
    )(scaled, projection.reshape(variants, RANK))


def solution(mesh):
    in_specs = (P("wide", "narrow"), P("narrow"), P("narrow"), P("narrow", None))
    out_specs = (P("wide", None), P("narrow", None))
    return jax.shard_map(body, mesh=mesh, in_specs=in_specs, out_specs=out_specs, check_vma=False)
```

```python
import functools

import jax
import jax.numpy as jnp
from jax import lax
from jax.experimental import pallas as pl
from jax.experimental.pallas import tpu as pltpu
from jax.sharding import PartitionSpec as P

NX, NY, NZ = 4, 4, 8
RANK = 128
SIZES = (4, 4, 4, 4)
CHUNKS = 4
EARLY = 3
LAG = 2
BLOCKS = 4
AHEAD = 5
PANEL = 16
F32, BF16 = jnp.float32, jnp.bfloat16
MESH = pl.DeviceIdType.MESH


class Place:
    def __init__(self):
        w = lax.axis_index("wide")
        self.w = w
        self.c = lax.axis_index("narrow")
        self.x = lax.rem(w, NX)
        self.z = lax.rem(lax.div(w, NX), NZ)
        self.y = lax.div(w, NX * NZ)
        self.p = self.y * NX + self.x

    def plane(self, dy, dx):
        yy, xx = lax.rem(self.y + dy, NY), lax.rem(self.x + dx, NX)
        return yy * NX + xx, {"wide": (yy * NZ + self.z) * NX + xx, "narrow": self.c}

    def column(self, dz):
        zz = lax.rem(self.z + dz, NZ)
        return zz, {"wide": (self.y * NZ + zz) * NX + self.x, "narrow": self.c}


def hops(d, n):
    return min(d, n - d)


def far_first(n):
    return sorted(range(n), key=lambda d: -hops(d, n))


def plane_steps():
    steps = [(dy * NX + dx, dy, dx) for dy in range(NY) for dx in range(NX)]
    return sorted(steps, key=lambda s: -hops(s[1], NY) - hops(s[2], NX))[:-1]


def remote(src, dst, send, recv, device):
    copy = pltpu.make_async_remote_copy(
        src_ref=src, dst_ref=dst, send_sem=send, recv_sem=recv, device_id=device, device_id_type=MESH
    )
    copy.start()
    return copy


def wait_bytes(ref, sem):
    pltpu.make_async_copy(ref, ref, sem).wait()


def split3(v):
    hi = v.astype(BF16)
    rest = v - hi.astype(F32)
    mid = rest.astype(BF16)
    low = (rest - mid.astype(F32)).astype(BF16)
    return hi, mid, low


def contract(a, b, dim):
    return lax.dot_general(a, b, (((dim,), (dim,)), ((), ())), preferred_element_type=F32)


def eliminate(aug, dinv, k):
    n = RANK
    base = k * PANEL
    prow = lax.broadcasted_iota(jnp.int32, (PANEL, n), 0)
    p = aug[base : base + PANEL, :]
    cols = [jnp.broadcast_to(p[:, base + j : base + j + 1], (PANEL, n)) for j in range(PANEL)]
    inv = jnp.zeros((PANEL, n), F32)
    for i in range(PANEL):
        ra = 1.0 / cols[i][i : i + 1, :]
        inv = jnp.where(prow == i, ra, inv)
        m = cols[i] * ra
        for j in range(i + 1, PANEL):
            cols[j] = cols[j] - m * cols[j][i : i + 1, :]
        m = jnp.where(prow > i, m, 0.0)
        p = p - jnp.concatenate([m, m], axis=1) * p[i : i + 1, :]
    aug[base : base + PANEL, n:] = p[:, n:]
    dinv[base : base + PANEL, :] = inv
    if base + PANEL < n:
        h, m, l = split3(p[:, :n])
        left = jnp.concatenate([h, h, m, h, l, m], axis=0)
        h, m, l = split3(p * jnp.concatenate([inv, inv], axis=1))
        right = jnp.concatenate([h, m, h, l, h, m], axis=0)
        upd = contract(left, right, 0)
        aug[base + PANEL :, :] = aug[base + PANEL :, :] - upd[base + PANEL :, :]


def basis_of(hm, low, factor):
    h, m, l = split3(factor)
    return contract(hm[...], jnp.concatenate([h, h], axis=1), 1) + (
        contract(hm[...], jnp.concatenate([m, m], axis=1), 1)
        + contract(jnp.concatenate([low[...], hm[:, :RANK]], axis=1), jnp.concatenate([h, l], axis=1), 1)
    )


def basis_t_of(hmt, lowt, factor):
    n = factor.shape[0]
    h, m, l = split3(factor)
    left = jnp.concatenate(
        [jnp.concatenate([h, h], axis=1), jnp.concatenate([m, m], axis=1), jnp.concatenate([l, jnp.zeros_like(l)], axis=1)],
        axis=0,
    )
    r = jnp.dot(left, hmt[...], preferred_element_type=F32)
    return r[:n] + (r[n : 2 * n] + (r[2 * n :] + jnp.dot(h, lowt[...], preferred_element_type=F32)))


def main_kernel(
    factor,
    gen, mean_hbm, scale_hbm, test_hbm, scaled, out,
    gbuf, mean, scale, test, std, part, other, hm, low, hmt, lowt,
    gm, r1, r2, total, aug, dinv, pm, pa, zb,
    gsem, osem, ps, pr, ss, rs, sa, va, sb, vb, sc, vc,
):
    me = Place()
    starts = [sum(SIZES[:k]) * gbuf.shape[0] // 16 for k in range(CHUNKS + 1)]
    chunks = [pl.ds(a, b - a) for a, b in zip(starts, starts[1:])]
    plane = NX * NY
    steps = plane_steps()
    partner = {"wide": me.w, "narrow": 1 - me.c}

    loads = []

    def load(first, last):
        for i in range(first, last):
            if i < 3:
                src, dst = ((mean_hbm, mean), (scale_hbm, scale), (test_hbm, test))[i]
                copy = pltpu.make_async_copy(src, dst, osem.at[i])
            else:
                at = chunks[i - 3]
                copy = pltpu.make_async_copy(gen.at[at], gbuf.at[at], gsem.at[i - 3])
            copy.start()
            loads.append(copy)

    load(0, AHEAD)
    barrier = pltpu.get_barrier_semaphore()
    peers = [(hops(dy, NY) + hops(dx, NX), me.plane(dy, dx)[1]) for _, dy, dx in steps]
    peers += [(hops(dz, NZ), me.column(dz)[1]) for dz in range(1, NZ)] + [(0, partner)]
    for _, device in sorted(peers, key=lambda p: -p[0]):
        pl.semaphore_signal(barrier, inc=1, device_id=device, device_id_type=MESH)
    load(AHEAD, 3 + CHUNKS)

    for copy in loads[:3]:
        copy.wait()
    pairs = []
    acc = [jnp.zeros((2 * RANK, 2 * RANK), F32), jnp.zeros((RANK, RANK), F32)]

    def exchange(k):
        at = chunks[k]
        pairs.append(remote(part.at[at], other.at[at], ps.at[k], pr.at[k], partner))

    def combine(k):
        at = chunks[k]
        pairs[k].wait_recv()
        s = part[at, :] + other[at, :]
        h, m, low[at, :] = split3(s)
        hm[at, :] = jnp.concatenate([h, m], axis=1)
        acc[0] += contract(hm[at, :], hm[at, :], 0)
        acc[1] += contract(low[at, :], h, 0)

    done = 0
    for k in range(CHUNKS):
        at = chunks[k]
        loads[3 + k].wait()
        x = ((gbuf[at, :].astype(F32) - mean[...]) * scale[...]).astype(BF16)
        std[at, :] = x
        part[at, :] = jnp.dot(x, test[...], preferred_element_type=F32)
        if k == EARLY - 1:
            pl.semaphore_wait(barrier, plane - 1 + NZ - 1 + 1)
            for i in range(EARLY):
                exchange(i)
        elif k >= EARLY:
            exchange(k)
            if k - done >= LAG:
                combine(done)
                done += 1
    while done < CHUNKS:
        combine(done)
        done += 1

    a, b = acc
    a = a[:RANK, :RANK] + ((a[:RANK, RANK:] + a[RANK:, :RANK]) + (a[RANK:, RANK:] + (b + b.T)))
    gm[...] = a.reshape(gm.shape)
    for s, dy, dx in steps:
        q, device = me.plane(dy, dx)
        remote(gm.at[q], r1.at[s], ss.at[0], rs.at[0], device)
    t = gm[me.p]
    for copy in pairs:
        copy.wait_send()
    wait_bytes(r1.at[pl.ds(1, plane - 1)], rs.at[0])
    for s in range(1, plane):
        t += r1[s]
    r2[me.z] = t
    for dz in far_first(NZ)[:-1]:
        _, device = me.column(dz)
        remote(r2.at[me.z], r2.at[me.z], ss.at[1], rs.at[1], device)
    wait_bytes(gm.at[pl.ds(0, plane - 1)], ss.at[0])
    wait_bytes(r2.at[pl.ds(0, NZ - 1)], rs.at[1])
    t = r2[0]
    for i in range(1, NZ):
        t += r2[i]
    total[me.p] = t
    for s, dy, dx in steps:
        _, device = me.plane(dy, dx)
        remote(total.at[me.p], total.at[me.p], ss.at[2], rs.at[2], device)
    wait_bytes(r2.at[pl.ds(0, NZ - 1)], ss.at[1])
    row = lax.broadcasted_iota(jnp.int32, (RANK, RANK), 0)
    col = lax.broadcasted_iota(jnp.int32, (RANK, RANK), 1)
    aug[:, RANK:] = jnp.where(row == col, 1.0, 0.0).astype(F32)
    hmt[...] = hm[...].T
    lowt[...] = low[...].T
    wait_bytes(total.at[pl.ds(0, plane - 1)], rs.at[2])
    wait_bytes(total.at[pl.ds(0, plane - 1)], ss.at[2])

    aug[:, :RANK] = total[...].reshape(RANK, RANK)
    half = RANK // 2
    parts = BLOCKS // 2
    width = std.shape[1] // parts
    grow = pm.shape[2]

    def project(hf):
        at = pl.ds(hf * half, half)
        factor = aug[at, RANK:] * jnp.sqrt(dinv[at, :])
        basis_low = basis_t_of(hmt, lowt, factor).astype(BF16)
        for b in range(parts):
            res = jnp.dot(basis_low, std[:, b * width : (b + 1) * width], preferred_element_type=F32)
            res = jnp.concatenate([res[:, : width // 2], res[:, width // 2 :]], axis=0)
            pm[hf * parts + b] = res.T.reshape(plane, grow, RANK)
            send(hf * parts + b)

    def send(i):
        for s, dy, dx in steps:
            q, device = me.plane(dy, dx)
            remote(pm.at[i, q], pa.at[i, s], sa.at[i], va.at[i], device)

    n_panels = RANK // PANEL
    for k in range(n_panels):
        eliminate(aug, dinv, k)
        if k == n_panels // 2 - 1:
            project(0)
    project(1)
    scaled[...] = basis_of(hm, low, aug[:, RANK:] * jnp.sqrt(dinv[...])) * factor

    for i in range(BLOCKS):
        t = pm[i, me.p]
        wait_bytes(pa.at[i, pl.ds(1, plane - 1)], va.at[i])
        for s in range(1, plane):
            t += pa[i, s]
        zb[i, me.z] = t
        for dz in far_first(NZ)[:-1]:
            _, device = me.column(dz)
            remote(zb.at[i, me.z], zb.at[i, me.z], sb.at[i], vb.at[i], device)
    for i in range(BLOCKS):
        wait_bytes(pm.at[i, pl.ds(0, plane - 1)], sa.at[i])
    for i in range(BLOCKS):
        wait_bytes(zb.at[i, pl.ds(0, NZ - 1)], vb.at[i])
        t = zb[i, 0]
        for z in range(1, NZ):
            t += zb[i, z]
        out[i, me.p] = t
        for s, dy, dx in steps:
            _, device = me.plane(dy, dx)
            remote(out.at[i, me.p], out.at[i, me.p], sc.at[i], vc.at[i], device)
    for i in range(BLOCKS):
        wait_bytes(zb.at[i, pl.ds(0, NZ - 1)], sb.at[i])
    for i in range(BLOCKS):
        wait_bytes(out.at[i, pl.ds(0, plane - 1)], sc.at[i])
        wait_bytes(out.at[i, pl.ds(0, plane - 1)], vc.at[i])


def place_kernel(scaled_in, blocks, scaled, projection, ordered, sems):
    copy = pltpu.make_async_copy(scaled_in, scaled, sems.at[0])
    copy.start()
    parts = BLOCKS // 2
    rows = blocks.shape[1] * blocks.shape[2]
    first = lax.broadcasted_iota(jnp.int32, (rows, RANK), 1) < RANK // 2
    for b in range(parts):
        lo, hi = (blocks[i].reshape(rows, RANK) for i in (b, parts + b))
        ordered[2 * b * rows : (2 * b + 1) * rows, :] = jnp.where(first, lo, pltpu.roll(hi, RANK // 2, 1))
        ordered[(2 * b + 1) * rows : (2 * b + 2) * rows, :] = jnp.where(first, pltpu.roll(lo, RANK // 2, 1), hi)
    last = pltpu.make_async_copy(ordered, projection, sems.at[1])
    last.start()
    copy.wait()
    last.wait()


def body(genotypes, allele_means, allele_scales, test_matrix):
    samples, variants = genotypes.shape
    plane = NX * NY
    dma = pltpu.SemaphoreType.DMA
    vmem = pl.BlockSpec(memory_space=pltpu.VMEM)
    piece = variants // (plane * BLOCKS)
    factor = float(samples * lax.axis_size("wide")) ** 0.5
    grow = RANK // plane
    operands = (genotypes, allele_means[None, :], allele_scales[None, :], test_matrix)
    operands = [pltpu.with_memory_space_constraint(v, pltpu.HBM) for v in operands]
    scaled, projection = pl.pallas_call(
        functools.partial(main_kernel, factor),
        out_shape=(
            jax.ShapeDtypeStruct((samples, RANK), F32),
            jax.ShapeDtypeStruct((BLOCKS, plane, piece, RANK), F32),
        ),
        in_specs=[pl.BlockSpec(memory_space=pltpu.HBM)] * 4,
        out_specs=(vmem, vmem),
        scratch_shapes=[
            pltpu.VMEM((samples, variants), jnp.int32),
            pltpu.VMEM((1, variants), F32),
            pltpu.VMEM((1, variants), F32),
            pltpu.VMEM((variants, RANK), BF16),
            pltpu.VMEM((samples, variants), BF16),
            pltpu.VMEM((samples, RANK), F32),
            pltpu.VMEM((samples, RANK), F32),
            pltpu.VMEM((samples, 2 * RANK), BF16),
            pltpu.VMEM((samples, RANK), BF16),
            pltpu.VMEM((2 * RANK, samples), BF16),
            pltpu.VMEM((RANK, samples), BF16),
            pltpu.VMEM((plane, grow, RANK), F32),
            pltpu.VMEM((plane, grow, RANK), F32),
            pltpu.VMEM((NZ, grow, RANK), F32),
            pltpu.VMEM((plane, grow, RANK), F32),
            pltpu.VMEM((RANK, 2 * RANK), F32),
            pltpu.VMEM((RANK, RANK), F32),
            pltpu.VMEM((BLOCKS, plane, piece, RANK), F32),
            pltpu.VMEM((BLOCKS, plane, piece, RANK), F32),
            pltpu.VMEM((BLOCKS, NZ, piece, RANK), F32),
            dma((CHUNKS,)), dma((3,)), dma((CHUNKS,)), dma((CHUNKS,)),
            dma((3,)), dma((3,)), dma((BLOCKS,)), dma((BLOCKS,)),
            dma((BLOCKS,)), dma((BLOCKS,)), dma((BLOCKS,)), dma((BLOCKS,)),
        ],
        compiler_params=pltpu.CompilerParams(
            collective_id=0, has_side_effects=True, vmem_limit_bytes=40 << 20
        ),
        name="sketch_factor_project",
    )(*operands)
    return pl.pallas_call(
        place_kernel,
        out_shape=(
            jax.ShapeDtypeStruct((samples, RANK), F32),
            jax.ShapeDtypeStruct((variants, RANK), F32),
        ),
        in_specs=[vmem, vmem],
        out_specs=(pl.BlockSpec(memory_space=pltpu.HBM), pl.BlockSpec(memory_space=pltpu.HBM)),
        scratch_shapes=[pltpu.VMEM((variants, RANK), F32), dma((2,))],
        compiler_params=pltpu.CompilerParams(vmem_limit_bytes=4 << 20),
        name="place",
    )(scaled, projection)


def solution(mesh):
    in_specs = (P("wide", "narrow"), P("narrow"), P("narrow"), P("narrow", None))
    out_specs = (P("wide", None), P("narrow", None))
    return jax.shard_map(body, mesh=mesh, in_specs=in_specs, out_specs=out_specs, check_vma=False)
```

```python
import functools

import jax
import jax.numpy as jnp
from jax import lax
from jax.experimental import pallas as pl
from jax.experimental.pallas import tpu as pltpu
from jax.sharding import PartitionSpec as P

NX, NY, NZ = 4, 4, 8
RANK = 128
SIZES = (4, 4, 4, 4)
CHUNKS = 4
EARLY = 3
LAG = 2
BLOCKS = 4
AHEAD = 5
PANEL = 16
F32, BF16 = jnp.float32, jnp.bfloat16
MESH = pl.DeviceIdType.MESH


class Place:
    def __init__(self):
        w = lax.axis_index("wide")
        self.w = w
        self.c = lax.axis_index("narrow")
        self.x = lax.rem(w, NX)
        self.z = lax.rem(lax.div(w, NX), NZ)
        self.y = lax.div(w, NX * NZ)
        self.p = self.y * NX + self.x

    def plane(self, dy, dx):
        yy, xx = lax.rem(self.y + dy, NY), lax.rem(self.x + dx, NX)
        return yy * NX + xx, {"wide": (yy * NZ + self.z) * NX + xx, "narrow": self.c}

    def column(self, dz):
        zz = lax.rem(self.z + dz, NZ)
        return zz, {"wide": (self.y * NZ + zz) * NX + self.x, "narrow": self.c}


def hops(d, n):
    return min(d, n - d)


def far_first(n):
    return sorted(range(n), key=lambda d: -hops(d, n))


def plane_steps():
    steps = [(dy * NX + dx, dy, dx) for dy in range(NY) for dx in range(NX)]
    return sorted(steps, key=lambda s: -hops(s[1], NY) - hops(s[2], NX))[:-1]


def remote(src, dst, send, recv, device):
    copy = pltpu.make_async_remote_copy(
        src_ref=src, dst_ref=dst, send_sem=send, recv_sem=recv, device_id=device, device_id_type=MESH
    )
    copy.start()
    return copy


def wait_bytes(ref, sem):
    pltpu.make_async_copy(ref, ref, sem).wait()


def split3(v):
    hi = v.astype(BF16)
    rest = v - hi.astype(F32)
    mid = rest.astype(BF16)
    low = (rest - mid.astype(F32)).astype(BF16)
    return hi, mid, low


def contract(a, b, dim):
    return lax.dot_general(a, b, (((dim,), (dim,)), ((), ())), preferred_element_type=F32)


def eliminate(aug, dinv, k):
    n = RANK
    base = k * PANEL
    row = lax.broadcasted_iota(jnp.int32, (8, n), 0)
    rows = range(PANEL // 8)
    g = [aug[base + 8 * t : base + 8 * t + 8, :n] for t in rows]
    w = [aug[base + 8 * t : base + 8 * t + 8, n:] for t in rows]
    cols = [[jnp.broadcast_to(v[:, base + j : base + j + 1], (8, n)) for j in range(PANEL)] for v in g]
    inv = [jnp.zeros((8, n), F32) for _ in rows]
    for i in range(PANEL):
        top, r = divmod(i, 8)
        ra = 1.0 / cols[top][i][r : r + 1, :]
        inv[top] = jnp.where(row == r, ra, inv[top])
        m = {t: cols[t][i] * ra for t in rows[top:]}
        for j in range(i + 1, PANEL):
            pivot_row = cols[top][j][r : r + 1, :]
            for t in rows[top:]:
                cols[t][j] = cols[t][j] - m[t] * pivot_row
        m[top] = jnp.where(row > r, m[top], 0.0)
        g_row, w_row = g[top][r : r + 1, :], w[top][r : r + 1, :]
        for t in rows[top:]:
            g[t], w[t] = g[t] - m[t] * g_row, w[t] - m[t] * w_row
    g, w, inv = (jnp.concatenate(v, axis=0) for v in (g, w, inv))
    aug[base : base + PANEL, n:] = w
    dinv[base : base + PANEL, :] = inv
    if base + PANEL < n:
        h, m, l = split3(g)
        left = jnp.concatenate([h, h, m, h, l, m], axis=0).T
        h, m, l = split3(jnp.concatenate([g * inv, w * inv], axis=1))
        right = jnp.concatenate([h, m, h, l, h, m], axis=0)
        for first, last in ((base + PANEL, base + 2 * PANEL), (base + 2 * PANEL, n)):
            if first < last:
                upd = jnp.dot(left[first:last], right, preferred_element_type=F32)
                aug[first:last, :] = aug[first:last, :] - upd


def basis_of(hm, low, factor):
    h, m, l = split3(factor)
    return contract(hm[...], jnp.concatenate([h, h], axis=1), 1) + (
        contract(hm[...], jnp.concatenate([m, m], axis=1), 1)
        + contract(jnp.concatenate([low[...], hm[:, :RANK]], axis=1), jnp.concatenate([h, l], axis=1), 1)
    )


def basis_t_of(hmt, lowt, factor):
    n = factor.shape[0]
    h, m, l = split3(factor)
    left = jnp.concatenate(
        [jnp.concatenate([h, h], axis=1), jnp.concatenate([m, m], axis=1), jnp.concatenate([l, jnp.zeros_like(l)], axis=1)],
        axis=0,
    )
    r = jnp.dot(left, hmt[...], preferred_element_type=F32)
    return r[:n] + (r[n : 2 * n] + (r[2 * n :] + jnp.dot(h, lowt[...], preferred_element_type=F32)))


def main_kernel(
    factor,
    gen, mean_hbm, scale_hbm, test_hbm, scaled, out,
    gbuf, mean, scale, test, std, part, other, hm, low, hmt, lowt,
    gm, r1, r2, total, aug, dinv, pm, pa, zb,
    gsem, osem, ps, pr, ss, rs, sa, va, sb, vb, sc, vc,
):
    me = Place()
    starts = [sum(SIZES[:k]) * gbuf.shape[0] // 16 for k in range(CHUNKS + 1)]
    chunks = [pl.ds(a, b - a) for a, b in zip(starts, starts[1:])]
    plane = NX * NY
    steps = plane_steps()
    partner = {"wide": me.w, "narrow": 1 - me.c}

    loads = []

    def load(first, last):
        for i in range(first, last):
            if i < 3:
                src, dst = ((mean_hbm, mean), (scale_hbm, scale), (test_hbm, test))[i]
                copy = pltpu.make_async_copy(src, dst, osem.at[i])
            else:
                at = chunks[i - 3]
                copy = pltpu.make_async_copy(gen.at[at], gbuf.at[at], gsem.at[i - 3])
            copy.start()
            loads.append(copy)

    load(0, AHEAD)
    barrier = pltpu.get_barrier_semaphore()
    peers = [(hops(dy, NY) + hops(dx, NX), me.plane(dy, dx)[1]) for _, dy, dx in steps]
    peers += [(hops(dz, NZ), me.column(dz)[1]) for dz in range(1, NZ)] + [(0, partner)]
    for _, device in sorted(peers, key=lambda p: -p[0]):
        pl.semaphore_signal(barrier, inc=1, device_id=device, device_id_type=MESH)
    load(AHEAD, 3 + CHUNKS)

    for copy in loads[:3]:
        copy.wait()
    pairs = []
    acc = [jnp.zeros((2 * RANK, 2 * RANK), F32), jnp.zeros((RANK, RANK), F32)]

    def exchange(k):
        at = chunks[k]
        pairs.append(remote(part.at[at], other.at[at], ps.at[k], pr.at[k], partner))

    def combine(k):
        at = chunks[k]
        pairs[k].wait_recv()
        s = part[at, :] + other[at, :]
        h, m, low[at, :] = split3(s)
        hm[at, :] = jnp.concatenate([h, m], axis=1)
        acc[0] += contract(hm[at, :], hm[at, :], 0)
        acc[1] += contract(low[at, :], h, 0)

    done = 0
    for k in range(CHUNKS):
        at = chunks[k]
        loads[3 + k].wait()
        x = ((gbuf[at, :].astype(F32) - mean[...]) * scale[...]).astype(BF16)
        std[at, :] = x
        part[at, :] = jnp.dot(x, test[...], preferred_element_type=F32)
        if k == EARLY - 1:
            pl.semaphore_wait(barrier, plane - 1 + NZ - 1 + 1)
            for i in range(EARLY):
                exchange(i)
        elif k >= EARLY:
            exchange(k)
            if k - done >= LAG:
                combine(done)
                done += 1
    while done < CHUNKS:
        combine(done)
        done += 1

    a, b = acc
    a = a[:RANK, :RANK] + ((a[:RANK, RANK:] + a[RANK:, :RANK]) + (a[RANK:, RANK:] + (b + b.T)))
    gm[...] = a.reshape(gm.shape)
    for s, dy, dx in steps:
        q, device = me.plane(dy, dx)
        remote(gm.at[q], r1.at[s], ss.at[0], rs.at[0], device)
    t = gm[me.p]
    for copy in pairs:
        copy.wait_send()
    wait_bytes(r1.at[pl.ds(1, plane - 1)], rs.at[0])
    for s in range(1, plane):
        t += r1[s]
    r2[me.z] = t
    for dz in far_first(NZ)[:-1]:
        _, device = me.column(dz)
        remote(r2.at[me.z], r2.at[me.z], ss.at[1], rs.at[1], device)
    wait_bytes(gm.at[pl.ds(0, plane - 1)], ss.at[0])
    wait_bytes(r2.at[pl.ds(0, NZ - 1)], rs.at[1])
    t = r2[0]
    for i in range(1, NZ):
        t += r2[i]
    total[me.p] = t
    for s, dy, dx in steps:
        _, device = me.plane(dy, dx)
        remote(total.at[me.p], total.at[me.p], ss.at[2], rs.at[2], device)
    wait_bytes(r2.at[pl.ds(0, NZ - 1)], ss.at[1])
    row = lax.broadcasted_iota(jnp.int32, (RANK, RANK), 0)
    col = lax.broadcasted_iota(jnp.int32, (RANK, RANK), 1)
    aug[:, RANK:] = jnp.where(row == col, 1.0, 0.0).astype(F32)
    hmt[...] = hm[...].T
    lowt[...] = low[...].T
    wait_bytes(total.at[pl.ds(0, plane - 1)], rs.at[2])
    wait_bytes(total.at[pl.ds(0, plane - 1)], ss.at[2])

    aug[:, :RANK] = total[...].reshape(RANK, RANK)
    half = RANK // 2
    parts = BLOCKS // 2
    width = std.shape[1] // parts
    grow = pm.shape[2]

    def project(hf):
        at = pl.ds(hf * half, half)
        factor = aug[at, RANK:] * jnp.sqrt(dinv[at, :])
        basis_low = basis_t_of(hmt, lowt, factor).astype(BF16)
        for b in range(parts):
            res = jnp.dot(basis_low, std[:, b * width : (b + 1) * width], preferred_element_type=F32)
            res = jnp.concatenate([res[:, : width // 2], res[:, width // 2 :]], axis=0)
            pm[hf * parts + b] = res.T.reshape(plane, grow, RANK)
            send(hf * parts + b)

    def send(i):
        for s, dy, dx in steps:
            q, device = me.plane(dy, dx)
            remote(pm.at[i, q], pa.at[i, s], sa.at[i], va.at[i], device)

    n_panels = RANK // PANEL
    for k in range(n_panels):
        eliminate(aug, dinv, k)
        if k == n_panels // 2 - 1:
            project(0)
    project(1)
    for i in range(BLOCKS):
        t = pm[i, me.p]
        wait_bytes(pa.at[i, pl.ds(1, plane - 1)], va.at[i])
        for s in range(1, plane):
            t += pa[i, s]
        zb[i, me.z] = t
        for dz in far_first(NZ)[:-1]:
            _, device = me.column(dz)
            remote(zb.at[i, me.z], zb.at[i, me.z], sb.at[i], vb.at[i], device)
    scaled[...] = basis_of(hm, low, aug[:, RANK:] * jnp.sqrt(dinv[...])) * factor
    for i in range(BLOCKS):
        wait_bytes(pm.at[i, pl.ds(0, plane - 1)], sa.at[i])
    for i in range(BLOCKS):
        wait_bytes(zb.at[i, pl.ds(0, NZ - 1)], vb.at[i])
        t = zb[i, 0]
        for z in range(1, NZ):
            t += zb[i, z]
        out[i, me.p] = t
        for s, dy, dx in steps:
            _, device = me.plane(dy, dx)
            remote(out.at[i, me.p], out.at[i, me.p], sc.at[i], vc.at[i], device)
    for i in range(BLOCKS):
        wait_bytes(zb.at[i, pl.ds(0, NZ - 1)], sb.at[i])
    for i in range(BLOCKS):
        wait_bytes(out.at[i, pl.ds(0, plane - 1)], sc.at[i])
        wait_bytes(out.at[i, pl.ds(0, plane - 1)], vc.at[i])


def place_kernel(scaled_in, blocks, scaled, projection, ordered, sems):
    copy = pltpu.make_async_copy(scaled_in, scaled, sems.at[0])
    copy.start()
    parts = BLOCKS // 2
    rows = blocks.shape[1] * blocks.shape[2]
    first = lax.broadcasted_iota(jnp.int32, (rows, RANK), 1) < RANK // 2
    for b in range(parts):
        lo, hi = (blocks[i].reshape(rows, RANK) for i in (b, parts + b))
        ordered[2 * b * rows : (2 * b + 1) * rows, :] = jnp.where(first, lo, pltpu.roll(hi, RANK // 2, 1))
        ordered[(2 * b + 1) * rows : (2 * b + 2) * rows, :] = jnp.where(first, pltpu.roll(lo, RANK // 2, 1), hi)
    last = pltpu.make_async_copy(ordered, projection, sems.at[1])
    last.start()
    copy.wait()
    last.wait()


def body(genotypes, allele_means, allele_scales, test_matrix):
    samples, variants = genotypes.shape
    plane = NX * NY
    dma = pltpu.SemaphoreType.DMA
    vmem = pl.BlockSpec(memory_space=pltpu.VMEM)
    piece = variants // (plane * BLOCKS)
    factor = float(samples * lax.axis_size("wide")) ** 0.5
    grow = RANK // plane
    operands = (genotypes, allele_means[None, :], allele_scales[None, :], test_matrix)
    operands = [pltpu.with_memory_space_constraint(v, pltpu.HBM) for v in operands]
    scaled, projection = pl.pallas_call(
        functools.partial(main_kernel, factor),
        out_shape=(
            jax.ShapeDtypeStruct((samples, RANK), F32),
            jax.ShapeDtypeStruct((BLOCKS, plane, piece, RANK), F32),
        ),
        in_specs=[pl.BlockSpec(memory_space=pltpu.HBM)] * 4,
        out_specs=(vmem, vmem),
        scratch_shapes=[
            pltpu.VMEM((samples, variants), jnp.int32),
            pltpu.VMEM((1, variants), F32),
            pltpu.VMEM((1, variants), F32),
            pltpu.VMEM((variants, RANK), BF16),
            pltpu.VMEM((samples, variants), BF16),
            pltpu.VMEM((samples, RANK), F32),
            pltpu.VMEM((samples, RANK), F32),
            pltpu.VMEM((samples, 2 * RANK), BF16),
            pltpu.VMEM((samples, RANK), BF16),
            pltpu.VMEM((2 * RANK, samples), BF16),
            pltpu.VMEM((RANK, samples), BF16),
            pltpu.VMEM((plane, grow, RANK), F32),
            pltpu.VMEM((plane, grow, RANK), F32),
            pltpu.VMEM((NZ, grow, RANK), F32),
            pltpu.VMEM((plane, grow, RANK), F32),
            pltpu.VMEM((RANK, 2 * RANK), F32),
            pltpu.VMEM((RANK, RANK), F32),
            pltpu.VMEM((BLOCKS, plane, piece, RANK), F32),
            pltpu.VMEM((BLOCKS, plane, piece, RANK), F32),
            pltpu.VMEM((BLOCKS, NZ, piece, RANK), F32),
            dma((CHUNKS,)), dma((3,)), dma((CHUNKS,)), dma((CHUNKS,)),
            dma((3,)), dma((3,)), dma((BLOCKS,)), dma((BLOCKS,)),
            dma((BLOCKS,)), dma((BLOCKS,)), dma((BLOCKS,)), dma((BLOCKS,)),
        ],
        compiler_params=pltpu.CompilerParams(
            collective_id=0, has_side_effects=True, vmem_limit_bytes=40 << 20
        ),
        name="sketch_factor_project",
    )(*operands)
    return pl.pallas_call(
        place_kernel,
        out_shape=(
            jax.ShapeDtypeStruct((samples, RANK), F32),
            jax.ShapeDtypeStruct((variants, RANK), F32),
        ),
        in_specs=[vmem, vmem],
        out_specs=(pl.BlockSpec(memory_space=pltpu.HBM), pl.BlockSpec(memory_space=pltpu.HBM)),
        scratch_shapes=[pltpu.VMEM((variants, RANK), F32), dma((2,))],
        compiler_params=pltpu.CompilerParams(vmem_limit_bytes=4 << 20),
        name="place",
    )(scaled, projection)


def solution(mesh):
    in_specs = (P("wide", "narrow"), P("narrow"), P("narrow"), P("narrow", None))
    out_specs = (P("wide", None), P("narrow", None))
    return jax.shard_map(body, mesh=mesh, in_specs=in_specs, out_specs=out_specs, check_vma=False)
```

```python
import functools

import jax
import jax.numpy as jnp
from jax import lax
from jax.experimental import pallas as pl
from jax.experimental.pallas import tpu as pltpu
from jax.sharding import PartitionSpec as P

NX, NY, NZ = 4, 4, 8
RANK = 128
SIZES = (4, 4, 4, 4)
CHUNKS = 4
EARLY = 3
LAG = 2
BLOCKS = 8
AHEAD = 5
PANEL = 16
F32, BF16 = jnp.float32, jnp.bfloat16
MESH = pl.DeviceIdType.MESH


class Place:
    def __init__(self):
        w = lax.axis_index("wide")
        self.w = w
        self.c = lax.axis_index("narrow")
        self.x = lax.rem(w, NX)
        self.z = lax.rem(lax.div(w, NX), NZ)
        self.y = lax.div(w, NX * NZ)
        self.p = self.y * NX + self.x

    def plane(self, dy, dx):
        yy, xx = lax.rem(self.y + dy, NY), lax.rem(self.x + dx, NX)
        return yy * NX + xx, {"wide": (yy * NZ + self.z) * NX + xx, "narrow": self.c}

    def column(self, dz):
        zz = lax.rem(self.z + dz, NZ)
        return zz, {"wide": (self.y * NZ + zz) * NX + self.x, "narrow": self.c}


def hops(d, n):
    return min(d, n - d)


def far_first(n):
    return sorted(range(n), key=lambda d: -hops(d, n))


def plane_steps():
    steps = [(dy * NX + dx, dy, dx) for dy in range(NY) for dx in range(NX)]
    return sorted(steps, key=lambda s: -hops(s[1], NY) - hops(s[2], NX))[:-1]


def remote(src, dst, send, recv, device):
    copy = pltpu.make_async_remote_copy(
        src_ref=src, dst_ref=dst, send_sem=send, recv_sem=recv, device_id=device, device_id_type=MESH
    )
    copy.start()
    return copy


def wait_bytes(ref, sem):
    pltpu.make_async_copy(ref, ref, sem).wait()


def split3(v):
    hi = v.astype(BF16)
    rest = v - hi.astype(F32)
    mid = rest.astype(BF16)
    low = (rest - mid.astype(F32)).astype(BF16)
    return hi, mid, low


def contract(a, b, dim):
    return lax.dot_general(a, b, (((dim,), (dim,)), ((), ())), preferred_element_type=F32)


def eliminate(aug, dinv, k):
    n = RANK
    base = k * PANEL
    row = lax.broadcasted_iota(jnp.int32, (8, n), 0)
    rows = range(PANEL // 8)
    g = [aug[base + 8 * t : base + 8 * t + 8, :n] for t in rows]
    w = [aug[base + 8 * t : base + 8 * t + 8, n:] for t in rows]
    cols = [[jnp.broadcast_to(v[:, base + j : base + j + 1], (8, n)) for j in range(PANEL)] for v in g]
    inv = [jnp.zeros((8, n), F32) for _ in rows]
    for i in range(PANEL):
        top, r = divmod(i, 8)
        ra = 1.0 / cols[top][i][r : r + 1, :]
        inv[top] = jnp.where(row == r, ra, inv[top])
        m = {t: cols[t][i] * ra for t in rows[top:]}
        for j in range(i + 1, PANEL):
            pivot_row = cols[top][j][r : r + 1, :]
            for t in rows[top:]:
                cols[t][j] = cols[t][j] - m[t] * pivot_row
        m[top] = jnp.where(row > r, m[top], 0.0)
        g_row, w_row = g[top][r : r + 1, :], w[top][r : r + 1, :]
        for t in rows[top:]:
            g[t], w[t] = g[t] - m[t] * g_row, w[t] - m[t] * w_row
    g, w, inv = (jnp.concatenate(v, axis=0) for v in (g, w, inv))
    aug[base : base + PANEL, n:] = w
    dinv[base : base + PANEL, :] = inv
    if base + PANEL < n:
        h, m, l = split3(g)
        left = jnp.concatenate([h, h, m, h, l, m], axis=0).T
        h, m, l = split3(jnp.concatenate([g * inv, w * inv], axis=1))
        right = jnp.concatenate([h, m, h, l, h, m], axis=0)
        for first, last in ((base + PANEL, base + 2 * PANEL), (base + 2 * PANEL, n)):
            if first < last:
                upd = jnp.dot(left[first:last], right, preferred_element_type=F32)
                aug[first:last, :] = aug[first:last, :] - upd


def basis_of(hm, low, factor):
    h, m, l = split3(factor)
    return contract(hm[...], jnp.concatenate([h, h], axis=1), 1) + (
        contract(hm[...], jnp.concatenate([m, m], axis=1), 1)
        + contract(jnp.concatenate([low[...], hm[:, :RANK]], axis=1), jnp.concatenate([h, l], axis=1), 1)
    )


def basis_t_of(hmt, lowt, factor):
    n = factor.shape[0]
    h, m, l = split3(factor)
    left = jnp.concatenate(
        [jnp.concatenate([h, h], axis=1), jnp.concatenate([m, m], axis=1), jnp.concatenate([l, jnp.zeros_like(l)], axis=1)],
        axis=0,
    )
    r = jnp.dot(left, hmt[...], preferred_element_type=F32)
    return r[:n] + (r[n : 2 * n] + (r[2 * n :] + jnp.dot(h, lowt[...], preferred_element_type=F32)))


def main_kernel(
    factor,
    gen, mean_hbm, scale_hbm, test_hbm, scaled, out,
    gbuf, mean, scale, test, std, part, other, hm, low, hmt, lowt,
    gm, r1, r2, total, aug, dinv, pm, pa, zb,
    gsem, osem, ps, pr, ss, rs, sa, va, sb, vb, sc, vc,
):
    me = Place()
    starts = [sum(SIZES[:k]) * gbuf.shape[0] // 16 for k in range(CHUNKS + 1)]
    chunks = [pl.ds(a, b - a) for a, b in zip(starts, starts[1:])]
    plane = NX * NY
    steps = plane_steps()
    partner = {"wide": me.w, "narrow": 1 - me.c}

    loads = []

    def load(first, last):
        for i in range(first, last):
            if i < 3:
                src, dst = ((mean_hbm, mean), (scale_hbm, scale), (test_hbm, test))[i]
                copy = pltpu.make_async_copy(src, dst, osem.at[i])
            else:
                at = chunks[i - 3]
                copy = pltpu.make_async_copy(gen.at[at], gbuf.at[at], gsem.at[i - 3])
            copy.start()
            loads.append(copy)

    load(0, AHEAD)
    barrier = pltpu.get_barrier_semaphore()
    peers = [(hops(dy, NY) + hops(dx, NX), me.plane(dy, dx)[1]) for _, dy, dx in steps]
    peers += [(hops(dz, NZ), me.column(dz)[1]) for dz in range(1, NZ)] + [(0, partner)]
    for _, device in sorted(peers, key=lambda p: -p[0]):
        pl.semaphore_signal(barrier, inc=1, device_id=device, device_id_type=MESH)
    load(AHEAD, 3 + CHUNKS)

    for copy in loads[:3]:
        copy.wait()
    pairs = []
    acc = [jnp.zeros((2 * RANK, 2 * RANK), F32), jnp.zeros((RANK, RANK), F32)]

    def exchange(k):
        at = chunks[k]
        pairs.append(remote(part.at[at], other.at[at], ps.at[k], pr.at[k], partner))

    def combine(k):
        at = chunks[k]
        pairs[k].wait_recv()
        s = part[at, :] + other[at, :]
        h, m, low[at, :] = split3(s)
        hm[at, :] = jnp.concatenate([h, m], axis=1)
        acc[0] += contract(hm[at, :], hm[at, :], 0)
        acc[1] += contract(low[at, :], h, 0)

    done = 0
    for k in range(CHUNKS):
        at = chunks[k]
        loads[3 + k].wait()
        x = ((gbuf[at, :].astype(F32) - mean[...]) * scale[...]).astype(BF16)
        std[at, :] = x
        part[at, :] = jnp.dot(x, test[...], preferred_element_type=F32)
        if k == EARLY - 1:
            pl.semaphore_wait(barrier, plane - 1 + NZ - 1 + 1)
            for i in range(EARLY):
                exchange(i)
        elif k >= EARLY:
            exchange(k)
            if k - done >= LAG:
                combine(done)
                done += 1
    while done < CHUNKS:
        combine(done)
        done += 1

    a, b = acc
    a = a[:RANK, :RANK] + ((a[:RANK, RANK:] + a[RANK:, :RANK]) + (a[RANK:, RANK:] + (b + b.T)))
    gm[...] = a.reshape(gm.shape)
    for s, dy, dx in steps:
        q, device = me.plane(dy, dx)
        remote(gm.at[q], r1.at[s], ss.at[0], rs.at[0], device)
    t = gm[me.p]
    for copy in pairs:
        copy.wait_send()
    wait_bytes(r1.at[pl.ds(1, plane - 1)], rs.at[0])
    for s in range(1, plane):
        t += r1[s]
    r2[me.z] = t
    for dz in far_first(NZ)[:-1]:
        _, device = me.column(dz)
        remote(r2.at[me.z], r2.at[me.z], ss.at[1], rs.at[1], device)
    wait_bytes(gm.at[pl.ds(0, plane - 1)], ss.at[0])
    wait_bytes(r2.at[pl.ds(0, NZ - 1)], rs.at[1])
    t = r2[0]
    for i in range(1, NZ):
        t += r2[i]
    total[me.p] = t
    for s, dy, dx in steps:
        _, device = me.plane(dy, dx)
        remote(total.at[me.p], total.at[me.p], ss.at[2], rs.at[2], device)
    wait_bytes(r2.at[pl.ds(0, NZ - 1)], ss.at[1])
    row = lax.broadcasted_iota(jnp.int32, (RANK, RANK), 0)
    col = lax.broadcasted_iota(jnp.int32, (RANK, RANK), 1)
    aug[:, RANK:] = jnp.where(row == col, 1.0, 0.0).astype(F32)
    hmt[...] = hm[...].T
    lowt[...] = low[...].T
    wait_bytes(total.at[pl.ds(0, plane - 1)], rs.at[2])
    wait_bytes(total.at[pl.ds(0, plane - 1)], ss.at[2])

    aug[:, :RANK] = total[...].reshape(RANK, RANK)
    half = RANK // 2
    parts = BLOCKS // 2
    width = std.shape[1] // parts
    grow = pm.shape[2]

    def project(hf):
        at = pl.ds(hf * half, half)
        factor = aug[at, RANK:] * jnp.sqrt(dinv[at, :])
        basis_low = basis_t_of(hmt, lowt, factor).astype(BF16)
        for b in range(parts):
            res = jnp.dot(basis_low, std[:, b * width : (b + 1) * width], preferred_element_type=F32)
            res = jnp.concatenate([res[:, : width // 2], res[:, width // 2 :]], axis=0)
            pm[hf * parts + b] = res.T.reshape(plane, grow, RANK)
            send(hf * parts + b)

    def send(i):
        for s, dy, dx in steps:
            q, device = me.plane(dy, dx)
            remote(pm.at[i, q], pa.at[i, s], sa.at[i], va.at[i], device)

    n_panels = RANK // PANEL
    for k in range(n_panels):
        eliminate(aug, dinv, k)
        if k == n_panels // 2 - 1:
            project(0)
    project(1)
    for i in range(BLOCKS):
        t = pm[i, me.p]
        wait_bytes(pa.at[i, pl.ds(1, plane - 1)], va.at[i])
        for s in range(1, plane):
            t += pa[i, s]
        zb[i, me.z] = t
        for dz in far_first(NZ)[:-1]:
            _, device = me.column(dz)
            remote(zb.at[i, me.z], zb.at[i, me.z], sb.at[i], vb.at[i], device)
    scaled[...] = basis_of(hm, low, aug[:, RANK:] * jnp.sqrt(dinv[...])) * factor
    for i in range(BLOCKS):
        wait_bytes(pm.at[i, pl.ds(0, plane - 1)], sa.at[i])
    for i in range(BLOCKS):
        wait_bytes(zb.at[i, pl.ds(0, NZ - 1)], vb.at[i])
        t = zb[i, 0]
        for z in range(1, NZ):
            t += zb[i, z]
        out[i, me.p] = t
        for s, dy, dx in steps:
            _, device = me.plane(dy, dx)
            remote(out.at[i, me.p], out.at[i, me.p], sc.at[i], vc.at[i], device)
    for i in range(BLOCKS):
        wait_bytes(zb.at[i, pl.ds(0, NZ - 1)], sb.at[i])
    for i in range(BLOCKS):
        wait_bytes(out.at[i, pl.ds(0, plane - 1)], sc.at[i])
        wait_bytes(out.at[i, pl.ds(0, plane - 1)], vc.at[i])


def place_kernel(scaled_in, blocks, scaled, projection, ordered, sems):
    copy = pltpu.make_async_copy(scaled_in, scaled, sems.at[0])
    copy.start()
    parts = BLOCKS // 2
    rows = blocks.shape[1] * blocks.shape[2]
    first = lax.broadcasted_iota(jnp.int32, (rows, RANK), 1) < RANK // 2
    for b in range(parts):
        lo, hi = (blocks[i].reshape(rows, RANK) for i in (b, parts + b))
        ordered[2 * b * rows : (2 * b + 1) * rows, :] = jnp.where(first, lo, pltpu.roll(hi, RANK // 2, 1))
        ordered[(2 * b + 1) * rows : (2 * b + 2) * rows, :] = jnp.where(first, pltpu.roll(lo, RANK // 2, 1), hi)
    last = pltpu.make_async_copy(ordered, projection, sems.at[1])
    last.start()
    copy.wait()
    last.wait()


def body(genotypes, allele_means, allele_scales, test_matrix):
    samples, variants = genotypes.shape
    plane = NX * NY
    dma = pltpu.SemaphoreType.DMA
    vmem = pl.BlockSpec(memory_space=pltpu.VMEM)
    piece = variants // (plane * BLOCKS)
    factor = float(samples * lax.axis_size("wide")) ** 0.5
    grow = RANK // plane
    operands = (genotypes, allele_means[None, :], allele_scales[None, :], test_matrix)
    operands = [pltpu.with_memory_space_constraint(v, pltpu.HBM) for v in operands]
    scaled, projection = pl.pallas_call(
        functools.partial(main_kernel, factor),
        out_shape=(
            jax.ShapeDtypeStruct((samples, RANK), F32),
            jax.ShapeDtypeStruct((BLOCKS, plane, piece, RANK), F32),
        ),
        in_specs=[pl.BlockSpec(memory_space=pltpu.HBM)] * 4,
        out_specs=(vmem, vmem),
        scratch_shapes=[
            pltpu.VMEM((samples, variants), jnp.int32),
            pltpu.VMEM((1, variants), F32),
            pltpu.VMEM((1, variants), F32),
            pltpu.VMEM((variants, RANK), BF16),
            pltpu.VMEM((samples, variants), BF16),
            pltpu.VMEM((samples, RANK), F32),
            pltpu.VMEM((samples, RANK), F32),
            pltpu.VMEM((samples, 2 * RANK), BF16),
            pltpu.VMEM((samples, RANK), BF16),
            pltpu.VMEM((2 * RANK, samples), BF16),
            pltpu.VMEM((RANK, samples), BF16),
            pltpu.VMEM((plane, grow, RANK), F32),
            pltpu.VMEM((plane, grow, RANK), F32),
            pltpu.VMEM((NZ, grow, RANK), F32),
            pltpu.VMEM((plane, grow, RANK), F32),
            pltpu.VMEM((RANK, 2 * RANK), F32),
            pltpu.VMEM((RANK, RANK), F32),
            pltpu.VMEM((BLOCKS, plane, piece, RANK), F32),
            pltpu.VMEM((BLOCKS, plane, piece, RANK), F32),
            pltpu.VMEM((BLOCKS, NZ, piece, RANK), F32),
            dma((CHUNKS,)), dma((3,)), dma((CHUNKS,)), dma((CHUNKS,)),
            dma((3,)), dma((3,)), dma((BLOCKS,)), dma((BLOCKS,)),
            dma((BLOCKS,)), dma((BLOCKS,)), dma((BLOCKS,)), dma((BLOCKS,)),
        ],
        compiler_params=pltpu.CompilerParams(
            collective_id=0, has_side_effects=True, vmem_limit_bytes=40 << 20
        ),
        name="sketch_factor_project",
    )(*operands)
    return pl.pallas_call(
        place_kernel,
        out_shape=(
            jax.ShapeDtypeStruct((samples, RANK), F32),
            jax.ShapeDtypeStruct((variants, RANK), F32),
        ),
        in_specs=[vmem, vmem],
        out_specs=(pl.BlockSpec(memory_space=pltpu.HBM), pl.BlockSpec(memory_space=pltpu.HBM)),
        scratch_shapes=[pltpu.VMEM((variants, RANK), F32), dma((2,))],
        compiler_params=pltpu.CompilerParams(vmem_limit_bytes=4 << 20),
        name="place",
    )(scaled, projection)


def solution(mesh):
    in_specs = (P("wide", "narrow"), P("narrow"), P("narrow"), P("narrow", None))
    out_specs = (P("wide", None), P("narrow", None))
    return jax.shard_map(body, mesh=mesh, in_specs=in_specs, out_specs=out_specs, check_vma=False)
```
